512 devices in a mesh: row: 16 (over y, x_hi, core), col: 32 (over z, x_lo).
Axes of the slice: x: 4 (x_hi: 2, x_lo: 2; x = x_hi * 2 + x_lo), y: 4, z: 16, core: 2. Of those that a mesh axis runs over, the one named last changes fastest.
Arguments:
- features: bfloat16 [98304, 128], P(('col', 'row')), may hold values from -6 to 6
- weight: bfloat16 [128, 128], replicated, may hold values from -48 to 48
- block_values: bfloat16 [32768, 128, 128], P(('row', 'col')), may hold values from 0 to 1
- block_coords: int32 [32768, 2], P(('row', 'col')), may hold values from 0 to 47, as said below
- block_counts: int32 [512], P(('row', 'col')), may hold values from 1 to 64, as said below
Outputs:
- convolved: bfloat16 [98304, 128], P(('row', 'col'))
The draws below stay inside these ranges and needn't reach their ends.
Inputs may be any that keep to these rules, and one draw needn't show every extreme that they name: `block_coords`: within one device the pairs are distinct; the first entry is below 48, the second below 24. `block_counts`: some device has exactly 64 live slots.
All inputs are finite; a program needn't handle non-finite values.
Results may differ from the reference program's by a relative error of at most 0.0049.
Values may be sent and summed in bfloat16 or wider, within the bound.
No kernel may reach another device: no remote copies, remote signals or barrier semaphores. Data moves between devices by JAX's collectives and lax.ppermute only.
A program may use at most 64 MiB of HBM per device.

```python
import jax
import jax.numpy as jnp
from jax import lax

F = 128
BLK = 128
NODES = 98304
ROWBLK = 6144
COLBLK = 3072
SLOTS = 1152
MAXB = 64
BLOCKS = 32768
N_ROW = 16
N_COL = 32


def draw_block_coords(key, part):
    key = jax.random.fold_in(key, 11)
    keys = jax.random.split(key, N_ROW * N_COL)
    slots = jax.vmap(lambda one_key: jax.random.permutation(one_key, SLOTS)[:MAXB])(keys)
    col_blocks = COLBLK // BLK
    coords = jnp.stack([slots // col_blocks, slots % col_blocks], axis=-1)
    return coords.reshape(BLOCKS, 2).astype(jnp.int32)


def draw_block_counts(key, part):
    key = jax.random.fold_in(key, 12)
    first_key, second_key = jax.random.split(key)
    counts = jax.random.randint(first_key, (N_ROW * N_COL,), 1, MAXB + 1)
    busiest = jax.random.randint(second_key, (), 0, N_ROW * N_COL)
    counts = jnp.where(jnp.arange(N_ROW * N_COL) == busiest, MAXB, counts)
    return counts.astype(jnp.int32)


def shard_levels(stream_key, dims, shards, low, top_value):
    loudness = 1.0
    for position, parts in shards:
        heights = jax.random.uniform(jax.random.fold_in(jax.random.fold_in(stream_key, 6), position), (parts,), jnp.float32, low / len(shards), top_value / len(shards))
        loudness = loudness * jnp.repeat(jnp.exp(heights), dims[position] // parts).reshape((-1,) + (1,) * (len(dims) - 1 - position))
    return loudness


def normal_values(key, dims, scale, reach, pieces=(), kind=jnp.bfloat16):
    drawn = jax.random.normal(key, dims, jnp.float32) * scale
    if len(pieces) > 0:
        drawn = shard_levels(key, dims, pieces, -0.22, 0.18) * drawn
    return jnp.clip(drawn, min=-reach, max=reach).astype(kind)


def setup_inputs(seed: int = 0) -> dict:
    key_list = jax.random.split(jax.random.key(seed), 6)
    features = normal_values(key_list[0], (NODES, F), 1.0, 6.0, ((0, 512),))
    weight = normal_values(key_list[1], (F, F), 8.0, 48.0)
    block_values = jnp.clip(1.0 * jax.random.uniform(key_list[2], (BLOCKS, BLK, BLK), jnp.float32) ** shard_levels(key_list[2], (BLOCKS, BLK, BLK), ((0, 512),), -0.2, 0.2), 0.0, 1.0).astype(jnp.bfloat16)
    block_coords = draw_block_coords(jax.random.fold_in(key_list[5], 71), 0)
    block_counts = draw_block_counts(jax.random.fold_in(key_list[5], 71), 0)
    return {"features": features, "weight": weight, "block_values": block_values, "block_coords": block_coords, "block_counts": block_counts}


def reference(features, weight, block_values, block_coords, block_counts):
    devices = N_ROW * N_COL
    row_blocks = ROWBLK // BLK
    col_blocks = COLBLK // BLK
    values_all = block_values.reshape(devices, MAXB, BLK, BLK)
    coords_all = block_coords.reshape(devices, MAXB, 2).astype(jnp.int32)
    live_mask = (jnp.arange(MAXB)[None, :] < block_counts[:, None]).astype(jnp.float32)
    device_row = (jnp.arange(devices) // N_COL).astype(jnp.int32)
    device_col = (jnp.arange(devices) % N_COL).astype(jnp.int32)
    row_index = (device_row[:, None] * row_blocks + coords_all[..., 0]).astype(jnp.int32)
    col_index = (device_col[:, None] * col_blocks + coords_all[..., 1]).astype(jnp.int32)

    def block_sums(values):
        wide = values.astype(jnp.float32)
        return (lax.optimization_barrier(jnp.sum(wide, axis=2)), lax.optimization_barrier(jnp.sum(wide, axis=1)))
    row_sums, col_sums = lax.map(block_sums, values_all)
    row_sums = row_sums * live_mask[..., None]
    col_sums = col_sums * live_mask[..., None]
    row_total = jnp.zeros((NODES // BLK, BLK), jnp.float32).at[row_index.reshape(-1)].add(row_sums.reshape(-1, BLK))
    col_total = jnp.zeros((NODES // BLK, BLK), jnp.float32).at[col_index.reshape(-1)].add(col_sums.reshape(-1, BLK))
    row_degree = 1.0 + row_total.reshape(NODES)
    col_degree = 1.0 + col_total.reshape(NODES)
    transformed = jnp.dot(features, weight, preferred_element_type=jnp.float32)
    scaled = (transformed * lax.rsqrt(col_degree)[:, None]).astype(jnp.bfloat16)
    scaled_blocks = scaled.reshape(NODES // BLK, BLK, F)

    def accumulate(totals, device):
        selected = jnp.take(scaled_blocks, col_index[device], axis=0).astype(jnp.float32)
        contrib = jnp.einsum('bij,bjf->bif', values_all[device].astype(jnp.float32), selected)
        contrib = contrib * live_mask[device][:, None, None]
        return (totals.at[row_index[device]].add(contrib), None)
    totals, unused = lax.scan(accumulate, jnp.zeros((NODES // BLK, BLK, F), jnp.float32), jnp.arange(devices))
    result = totals.reshape(NODES, F) * lax.rsqrt(row_degree)[:, None]
    return jax.nn.relu(result).astype(jnp.bfloat16)
```

```python
import jax
import jax.numpy as jnp
from jax import lax
from jax.experimental import pallas as pl
from jax.experimental.pallas import tpu as pltpu
from jax.sharding import PartitionSpec as P

F = 128
BLK = 128
SLOTS = 64
ROW_BLOCKS = 48
COL_BLOCKS = 24
OWN = 192
N_ROW = 16
N_COL = 32
CHIPS = N_ROW // 2
NEAR = 4
FAR = N_COL // NEAR
HALF = 64
UNROLL = 8

GATHER_ROWS = OWN + 2 * COL_BLOCKS
NEAR_ROWS = FAR * OWN + 4 * FAR
FAR_ROWS = OWN + 16

CHIP_GROUPS = [[2 * m + core for m in range(CHIPS)] for core in range(2)]
NEAR_GROUPS = [[NEAR * far + near for near in range(NEAR)] for far in range(FAR)]
FAR_GROUPS = [[NEAR * far + near for far in range(FAR)] for near in range(NEAR)]

VMEM = pl.BlockSpec(memory_space=pltpu.VMEM)
SMEM = pl.BlockSpec(memory_space=pltpu.SMEM)
f32 = jnp.float32
bf16 = jnp.bfloat16


def split(value):
    high = value.astype(bf16).astype(f32)
    return high, value - high


def column_sums_kernel(counts, coords, values, features, out, sums, parts):
    sums[...] = jnp.zeros_like(sums)
    live = counts[0]

    @pl.loop(0, lax.div(live + UNROLL - 1, UNROLL))
    def _(group):
        for step in range(UNROLL):
            slot = group * UNROLL + step
            col = jnp.where(slot < live, coords[1, slot], COL_BLOCKS)
            sums[pl.ds(col, 1), :] += jnp.sum(values[slot].astype(f32), axis=0, keepdims=True)

    high, low = split(sums[:COL_BLOCKS])
    parts[:COL_BLOCKS] = high
    parts[COL_BLOCKS:] = low
    for m in range(CHIPS):
        out[m, :OWN] = features[...]
        out[m, OWN:] = parts[...].astype(bf16)


def aggregate_kernel(core, counts, coords, mine, other, weight, values, out, scales, scaled, total, row_sums):
    live = counts[0]
    sums = jnp.zeros((2 * COL_BLOCKS, BLK), f32)
    for m in range(CHIPS):
        sums += mine[m, OWN:].astype(f32) + other[m, OWN:].astype(f32)
    degree = 1.0 + (sums[:COL_BLOCKS] + sums[COL_BLOCKS:])
    scales[...] = jnp.zeros_like(scales)
    scales[:COL_BLOCKS] = lax.rsqrt(degree)
    scales[...] = scales[...].T

    def scale(pieces):
        for r in range(N_ROW):
            transformed = jnp.dot(pieces[r % 2][r // 2, :OWN], weight[...], preferred_element_type=f32)
            for part in range(OWN // HALF):
                h = r * (OWN // HALF) + part
                factor = scales[(h % 2) * HALF : (h % 2 + 1) * HALF, h // 2 : h // 2 + 1]
                rows = transformed[part * HALF : (part + 1) * HALF]
                scaled[h * HALF : (h + 1) * HALF] = (rows * factor).astype(bf16)

    @pl.when(core[0] == 0)
    def _():
        scale((mine, other))

    @pl.when(core[0] == 1)
    def _():
        scale((other, mine))

    total[...] = jnp.zeros_like(total)
    row_sums[...] = jnp.zeros_like(row_sums)
    lane = lax.broadcasted_iota(jnp.int32, (BLK, BLK), 1)

    @pl.loop(0, lax.div(live + UNROLL - 1, UNROLL))
    def _(group):
        rows, products = [], []
        sums = row_sums[...]
        for step in range(UNROLL):
            slot = group * UNROLL + step
            alive = slot < live
            row = jnp.where(alive, coords[0, slot], ROW_BLOCKS)
            col = jnp.where(alive, coords[1, slot], 0)
            picked = scaled[pl.ds(pl.multiple_of(col * BLK, BLK), BLK), :]
            block = values[slot]
            rows.append(row)
            products.append(jnp.dot(block, picked, preferred_element_type=f32))
            sums += jnp.dot(block, (lane == row).astype(f32).astype(bf16), preferred_element_type=f32)
        row_sums[...] = sums
        for row, product in zip(rows, products):
            total[pl.ds(pl.multiple_of(row * BLK, BLK), BLK), :] += product

    high, low = split(row_sums[...].T)
    for near in range(NEAR):
        for far in range(FAR):
            dest = far * NEAR + near
            out[near, far * OWN : (far + 1) * OWN] = total[dest * OWN : (dest + 1) * OWN].astype(bf16)
        picks = []
        for part in (high, low):
            for far in range(FAR):
                first = (far * NEAR + near) * OWN // BLK
                picks.append(part[first : first + 2])
        out[near, FAR * OWN :] = jnp.concatenate(picks, axis=0).astype(bf16)


def near_kernel(pieces, out):
    for far in range(FAR):
        rows = pieces[0, far * OWN : (far + 1) * OWN].astype(f32)
        for near in range(1, NEAR):
            rows += pieces[near, far * OWN : (far + 1) * OWN].astype(f32)
        out[far, :OWN] = rows.astype(bf16)
    sums = pieces[0, FAR * OWN :].astype(f32)
    for near in range(1, NEAR):
        sums += pieces[near, FAR * OWN :].astype(f32)
    high, low = split(sums[: 2 * FAR] + sums[2 * FAR :])
    for far in range(FAR):
        rows = [high[2 * far : 2 * far + 2], low[2 * far : 2 * far + 2], jnp.zeros((12, BLK), f32)]
        out[far, OWN:] = jnp.concatenate(rows, axis=0).astype(bf16)


def far_kernel(odd, pieces, out):
    rows = pieces[0].astype(f32)
    for far in range(1, FAR):
        rows += pieces[far].astype(f32)
    sums = rows[OWN : OWN + 8]
    degree = 1.0 + (sums[0:2] + sums[2:4])
    scale = jnp.concatenate([lax.rsqrt(degree), jnp.zeros((BLK - 2, BLK), f32)], axis=0).T
    halves = [scale[(h % 2) * HALF : (h % 2 + 1) * HALF, h // 2 : h // 2 + 1] for h in range(4)]
    for part in range(OWN // HALF):
        factor = jnp.where(odd[0] == 1, halves[part + 1], halves[part])
        piece = rows[part * HALF : (part + 1) * HALF] * factor
        out[part * HALF : (part + 1) * HALF] = jnp.maximum(piece, 0.0).astype(bf16)


def params():
    return pltpu.CompilerParams(vmem_limit_bytes=32 * 1024 * 1024)


def shards(features, weight, block_values, block_coords, block_counts):
    coords = block_coords.T
    core = (lax.axis_index("row") % 2).astype(jnp.int32).reshape(1)
    odd = (lax.axis_index("col") % 2).astype(jnp.int32).reshape(1)

    outgoing = pl.pallas_call(
        column_sums_kernel,
        out_shape=jax.ShapeDtypeStruct((CHIPS, GATHER_ROWS, F), bf16),
        in_specs=[SMEM, SMEM, VMEM, VMEM],
        out_specs=VMEM,
        scratch_shapes=[pltpu.VMEM((32, BLK), f32), pltpu.VMEM((2 * COL_BLOCKS, BLK), f32)],
        compiler_params=params(),
    )(block_counts, coords, block_values, features)
    mine = lax.all_to_all(outgoing, "row", 0, 0, axis_index_groups=CHIP_GROUPS, tiled=True)
    other = lax.ppermute(mine, "row", [(r, r ^ 1) for r in range(N_ROW)])

    partial = pl.pallas_call(
        aggregate_kernel,
        out_shape=jax.ShapeDtypeStruct((NEAR, NEAR_ROWS, F), bf16),
        in_specs=[SMEM, SMEM, SMEM, VMEM, VMEM, VMEM, VMEM],
        out_specs=VMEM,
        scratch_shapes=[
            pltpu.VMEM((BLK, BLK), f32),
            pltpu.VMEM((COL_BLOCKS * BLK, F), bf16),
            pltpu.VMEM(((ROW_BLOCKS + 1) * BLK, F), f32),
            pltpu.VMEM((BLK, BLK), f32),
        ],
        compiler_params=params(),
    )(core, block_counts, coords, mine, other, weight, block_values)
    partial = lax.all_to_all(partial, "col", 0, 0, axis_index_groups=NEAR_GROUPS, tiled=True)

    reduced = pl.pallas_call(
        near_kernel,
        out_shape=jax.ShapeDtypeStruct((FAR, FAR_ROWS, F), bf16),
        in_specs=[VMEM],
        out_specs=VMEM,
        compiler_params=params(),
    )(partial)
    reduced = lax.all_to_all(reduced, "col", 0, 0, axis_index_groups=FAR_GROUPS, tiled=True)

    return pl.pallas_call(
        far_kernel,
        out_shape=jax.ShapeDtypeStruct((OWN, F), bf16),
        in_specs=[SMEM, VMEM],
        out_specs=VMEM,
        compiler_params=params(),
    )(odd, reduced)


def solution(mesh):
    return jax.shard_map(
        shards,
        mesh=mesh,
        in_specs=(
            P(("col", "row"), None),
            P(),
            P(("row", "col"), None, None),
            P(("row", "col"), None),
            P(("row", "col")),
        ),
        out_specs=P(("row", "col"), None),
        check_vma=False,
    )
```

```python
import jax
import jax.numpy as jnp
from jax import lax
from jax.experimental import pallas as pl
from jax.experimental.pallas import tpu as pltpu
from jax.sharding import PartitionSpec as P

F = 128
BLK = 128
SLOTS = 64
ROW_BLOCKS = 48
COL_BLOCKS = 24
OWN = 192
N_ROW = 16
N_COL = 32
CHIPS = N_ROW // 2
NEAR = 4
FAR = N_COL // NEAR
HALF = 64
UNROLL = 8

GATHER_ROWS = OWN + 2 * COL_BLOCKS
NEAR_ROWS = FAR * OWN + 4 * FAR
FAR_ROWS = OWN + 8

CHIP_GROUPS = [[2 * m + core for m in range(CHIPS)] for core in range(2)]
NEAR_GROUPS = [[NEAR * far + near for near in range(NEAR)] for far in range(FAR)]
FAR_GROUPS = [[NEAR * far + near for far in range(FAR)] for near in range(NEAR)]

VMEM = pl.BlockSpec(memory_space=pltpu.VMEM)
SMEM = pl.BlockSpec(memory_space=pltpu.SMEM)
HBM = pl.BlockSpec(memory_space=pltpu.HBM)
f32 = jnp.float32
bf16 = jnp.bfloat16


def split(value):
    high = value.astype(bf16).astype(f32)
    return high, value - high


def column_sums_kernel(counts_in, coords_in, values_in, features_in, out, counts, coords, values, features, sums, parts, small_sems, sems):
    small = [
        pltpu.make_async_copy(counts_in, counts, small_sems.at[0]),
        pltpu.make_async_copy(coords_in, coords, small_sems.at[1]),
        pltpu.make_async_copy(features_in, features, small_sems.at[2]),
    ]
    for copy in small:
        copy.start()
    chunks = []
    for group in range(SLOTS // UNROLL):
        slots = pl.ds(group * UNROLL, UNROLL)
        chunks.append(pltpu.make_async_copy(values_in.at[slots], values.at[slots], sems.at[group]))
        chunks[-1].start()
    sums[...] = jnp.zeros_like(sums)
    small[2].wait()
    for m in range(CHIPS):
        out[m, :OWN] = features[...]
    small[0].wait()
    small[1].wait()
    live = counts[0]
    for group in range(SLOTS // UNROLL):
        chunks[group].wait()

        @pl.when(group * UNROLL < live)
        def _():
            for step in range(UNROLL):
                slot = group * UNROLL + step
                col = jnp.where(slot < live, coords[1, slot], COL_BLOCKS)
                sums[pl.ds(col, 1), :] += jnp.sum(values[slot].astype(f32), axis=0, keepdims=True)

    high, low = split(sums[:COL_BLOCKS])
    parts[:COL_BLOCKS] = high
    parts[COL_BLOCKS:] = low
    for m in range(CHIPS):
        out[m, OWN:] = parts[...].astype(bf16)


def aggregate_kernel(core, counts, coords, mine, other, weight, values, out, scales, scaled, total, row_sums):
    live = counts[0]
    sums = jnp.zeros((2 * COL_BLOCKS, BLK), f32)
    for m in range(CHIPS):
        sums += mine[m, OWN:].astype(f32) + other[m, OWN:].astype(f32)
    degree = 1.0 + (sums[:COL_BLOCKS] + sums[COL_BLOCKS:])
    scales[...] = jnp.zeros_like(scales)
    scales[:COL_BLOCKS] = lax.rsqrt(degree)
    scales[...] = scales[...].T

    def scale(pieces):
        for r in range(N_ROW):
            transformed = jnp.dot(pieces[r % 2][r // 2, :OWN], weight[...], preferred_element_type=f32)
            for part in range(OWN // HALF):
                h = r * (OWN // HALF) + part
                factor = scales[(h % 2) * HALF : (h % 2 + 1) * HALF, h // 2 : h // 2 + 1]
                rows = transformed[part * HALF : (part + 1) * HALF]
                scaled[h * HALF : (h + 1) * HALF] = (rows * factor).astype(bf16)

    @pl.when(core[0] == 0)
    def _():
        scale((mine, other))

    @pl.when(core[0] == 1)
    def _():
        scale((other, mine))

    total[...] = jnp.zeros_like(total)
    row_sums[...] = jnp.zeros_like(row_sums)
    lane = lax.broadcasted_iota(jnp.int32, (BLK, BLK), 1)

    @pl.loop(0, lax.div(live + UNROLL - 1, UNROLL))
    def _(group):
        rows, products = [], []
        sums = row_sums[...]
        for step in range(UNROLL):
            slot = group * UNROLL + step
            alive = slot < live
            row = jnp.where(alive, coords[0, slot], ROW_BLOCKS)
            col = jnp.where(alive, coords[1, slot], 0)
            picked = scaled[pl.ds(pl.multiple_of(col * BLK, BLK), BLK), :]
            block = values[slot]
            rows.append(row)
            products.append(jnp.dot(block, picked, preferred_element_type=f32))
            sums += jnp.dot(block, (lane == row).astype(f32).astype(bf16), preferred_element_type=f32)
        row_sums[...] = sums
        for row, product in zip(rows, products):
            total[pl.ds(pl.multiple_of(row * BLK, BLK), BLK), :] += product

    high, low = split(row_sums[...].T)
    for near in range(NEAR):
        for far in range(FAR):
            dest = far * NEAR + near
            out[near, far * OWN : (far + 1) * OWN] = total[dest * OWN : (dest + 1) * OWN].astype(bf16)
        picks = []
        for part in (high, low):
            for far in range(FAR):
                first = (far * NEAR + near) * OWN // BLK
                picks.append(part[first : first + 2])
        out[near, FAR * OWN :] = jnp.concatenate(picks, axis=0).astype(bf16)


def near_kernel(pieces, out):
    sums = pieces[0, FAR * OWN :].astype(f32)
    for near in range(1, NEAR):
        sums += pieces[near, FAR * OWN :].astype(f32)
    high, low = split(sums[: 2 * FAR] + sums[2 * FAR :])
    for far in range(FAR):
        rows = pieces[0, far * OWN : (far + 1) * OWN].astype(f32)
        for near in range(1, NEAR):
            rows += pieces[near, far * OWN : (far + 1) * OWN].astype(f32)
        pair = slice(2 * far, 2 * far + 2)
        tail = jnp.concatenate([high[pair], low[pair], jnp.zeros((4, BLK), f32)], axis=0)
        out[far] = jnp.concatenate([rows, tail], axis=0).astype(bf16)


def far_kernel(odd, pieces, out):
    rows = pieces[0].astype(f32)
    for far in range(1, FAR):
        rows += pieces[far].astype(f32)
    sums = rows[OWN : OWN + 8]
    degree = 1.0 + (sums[0:2] + sums[2:4])
    scale = jnp.concatenate([lax.rsqrt(degree), jnp.zeros((BLK - 2, BLK), f32)], axis=0).T
    halves = [scale[(h % 2) * HALF : (h % 2 + 1) * HALF, h // 2 : h // 2 + 1] for h in range(4)]
    for part in range(OWN // HALF):
        factor = jnp.where(odd[0] == 1, halves[part + 1], halves[part])
        piece = rows[part * HALF : (part + 1) * HALF] * factor
        out[part * HALF : (part + 1) * HALF] = jnp.maximum(piece, 0.0).astype(bf16)


def params(mebibytes=32):
    return pltpu.CompilerParams(vmem_limit_bytes=mebibytes * 1024 * 1024)


def shards(features, weight, block_values, block_coords, block_counts):
    coords = block_coords.T
    core = (lax.axis_index("row") % 2).astype(jnp.int32).reshape(1)
    odd = (lax.axis_index("col") % 2).astype(jnp.int32).reshape(1)

    outgoing = pl.pallas_call(
        column_sums_kernel,
        out_shape=jax.ShapeDtypeStruct((CHIPS, GATHER_ROWS, F), bf16),
        in_specs=[HBM, HBM, HBM, HBM],
        out_specs=VMEM,
        scratch_shapes=[
            pltpu.SMEM((1,), jnp.int32),
            pltpu.SMEM((2, SLOTS), jnp.int32),
            pltpu.VMEM((SLOTS, BLK, BLK), bf16),
            pltpu.VMEM((OWN, F), bf16),
            pltpu.VMEM((32, BLK), f32),
            pltpu.VMEM((2 * COL_BLOCKS, BLK), f32),
            pltpu.SemaphoreType.DMA((3,)),
            pltpu.SemaphoreType.DMA((SLOTS // UNROLL,)),
        ],
        compiler_params=params(60),
    )(block_counts, coords, block_values, features)
    mine = lax.all_to_all(outgoing, "row", 0, 0, axis_index_groups=CHIP_GROUPS, tiled=True)
    other = lax.ppermute(mine, "row", [(r, r ^ 1) for r in range(N_ROW)])

    partial = pl.pallas_call(
        aggregate_kernel,
        out_shape=jax.ShapeDtypeStruct((NEAR, NEAR_ROWS, F), bf16),
        in_specs=[SMEM, SMEM, SMEM, VMEM, VMEM, VMEM, VMEM],
        out_specs=VMEM,
        scratch_shapes=[
            pltpu.VMEM((BLK, BLK), f32),
            pltpu.VMEM((COL_BLOCKS * BLK, F), bf16),
            pltpu.VMEM(((ROW_BLOCKS + 1) * BLK, F), f32),
            pltpu.VMEM((BLK, BLK), f32),
        ],
        compiler_params=params(),
    )(core, block_counts, coords, mine, other, weight, block_values)
    partial = lax.all_to_all(partial, "col", 0, 0, axis_index_groups=NEAR_GROUPS, tiled=True)

    reduced = pl.pallas_call(
        near_kernel,
        out_shape=jax.ShapeDtypeStruct((FAR, FAR_ROWS, F), bf16),
        in_specs=[VMEM],
        out_specs=VMEM,
        compiler_params=params(),
    )(partial)
    reduced = lax.all_to_all(reduced, "col", 0, 0, axis_index_groups=FAR_GROUPS, tiled=True)

    return pl.pallas_call(
        far_kernel,
        out_shape=jax.ShapeDtypeStruct((OWN, F), bf16),
        in_specs=[SMEM, VMEM],
        out_specs=VMEM,
        compiler_params=params(),
    )(odd, reduced)


def solution(mesh):
    return jax.shard_map(
        shards,
        mesh=mesh,
        in_specs=(
            P(("col", "row"), None),
            P(),
            P(("row", "col"), None, None),
            P(("row", "col"), None),
            P(("row", "col")),
        ),
        out_specs=P(("row", "col"), None),
        check_vma=False,
    )
```

```python
import jax
import jax.numpy as jnp
from jax import lax
from jax.experimental import pallas as pl
from jax.experimental.pallas import tpu as pltpu
from jax.sharding import PartitionSpec as P

F = 128
BLK = 128
SLOTS = 64
ROW_BLOCKS = 48
COL_BLOCKS = 24
OWN = 192
N_ROW = 16
N_COL = 32
CHIPS = N_ROW // 2
NEAR = 4
FAR = N_COL // NEAR
HALF = 64
UNROLL = 8
BATCH = 16

GATHER_ROWS = OWN + 2 * COL_BLOCKS
NEAR_ROWS = FAR * OWN + 4 * FAR
FAR_ROWS = OWN + 8

CHIP_GROUPS = [[2 * m + core for m in range(CHIPS)] for core in range(2)]
NEAR_GROUPS = [[NEAR * far + near for near in range(NEAR)] for far in range(FAR)]
FAR_GROUPS = [[NEAR * far + near for far in range(FAR)] for near in range(NEAR)]

VMEM = pl.BlockSpec(memory_space=pltpu.VMEM)
SMEM = pl.BlockSpec(memory_space=pltpu.SMEM)
HBM = pl.BlockSpec(memory_space=pltpu.HBM)
f32 = jnp.float32
bf16 = jnp.bfloat16


def split(value):
    high = value.astype(bf16).astype(f32)
    return high, value - high


def column_sums_kernel(counts_in, coords_in, values_in, features_in, out, counts, coords, values, features, sums, parts, small_sems, sems):
    small = [
        pltpu.make_async_copy(counts_in, counts, small_sems.at[0]),
        pltpu.make_async_copy(coords_in, coords, small_sems.at[1]),
        pltpu.make_async_copy(features_in, features, small_sems.at[2]),
    ]
    for copy in small:
        copy.start()
    chunks = []
    for group in range(SLOTS // UNROLL):
        slots = pl.ds(group * UNROLL, UNROLL)
        chunks.append(pltpu.make_async_copy(values_in.at[slots], values.at[slots], sems.at[group]))
        chunks[-1].start()
    sums[...] = jnp.zeros_like(sums)
    small[2].wait()
    for m in range(CHIPS):
        out[m, :OWN] = features[...]
    small[0].wait()
    small[1].wait()
    live = counts[0]
    for group in range(SLOTS // UNROLL):
        chunks[group].wait()

        @pl.when(group * UNROLL < live)
        def _():
            for step in range(UNROLL):
                slot = group * UNROLL + step
                col = jnp.where(slot < live, coords[1, slot], COL_BLOCKS)
                sums[pl.ds(col, 1), :] += jnp.sum(values[slot].astype(f32), axis=0, keepdims=True)

    high, low = split(sums[:COL_BLOCKS])
    parts[:COL_BLOCKS] = high
    parts[COL_BLOCKS:] = low
    for m in range(CHIPS):
        out[m, OWN:] = parts[...].astype(bf16)


def row_sums_kernel(mine, counts, coords, values, out, sums):
    live = counts[0]
    sums[...] = jnp.zeros_like(sums)
    lane = lax.broadcasted_iota(jnp.int32, (BLK, BLK), 1)

    @pl.loop(0, lax.div(live + BATCH - 1, BATCH))
    def _(group):
        added = sums[...]
        for step in range(BATCH):
            slot = group * BATCH + step
            row = jnp.where(slot < live, coords[0, slot], ROW_BLOCKS)
            picked = (lane == row).astype(f32).astype(bf16)
            added += jnp.dot(values[slot], picked, preferred_element_type=f32)
        sums[...] = added

    high, low = split(sums[...].T)
    for near in range(NEAR):
        picks = []
        for part in (high, low):
            for far in range(FAR):
                first = (far * NEAR + near) * OWN // BLK
                picks.append(part[first : first + 2])
        out[near] = jnp.concatenate(picks, axis=0).astype(bf16)


def aggregate_kernel(core, counts, coords, mine, other, weight, values, row_sums, out, scales, scaled, total):
    live = counts[0]
    sums = jnp.zeros((2 * COL_BLOCKS, BLK), f32)
    for m in range(CHIPS):
        sums += mine[m, OWN:].astype(f32) + other[m, OWN:].astype(f32)
    degree = 1.0 + (sums[:COL_BLOCKS] + sums[COL_BLOCKS:])
    scales[...] = jnp.zeros_like(scales)
    scales[:COL_BLOCKS] = lax.rsqrt(degree)
    scales[...] = scales[...].T

    def scale(pieces):
        for r in range(N_ROW):
            transformed = jnp.dot(pieces[r % 2][r // 2, :OWN], weight[...], preferred_element_type=f32)
            for part in range(OWN // HALF):
                h = r * (OWN // HALF) + part
                factor = scales[(h % 2) * HALF : (h % 2 + 1) * HALF, h // 2 : h // 2 + 1]
                rows = transformed[part * HALF : (part + 1) * HALF]
                scaled[h * HALF : (h + 1) * HALF] = (rows * factor).astype(bf16)

    @pl.when(core[0] == 0)
    def _():
        scale((mine, other))

    @pl.when(core[0] == 1)
    def _():
        scale((other, mine))

    total[...] = jnp.zeros_like(total)

    @pl.loop(0, lax.div(live + BATCH - 1, BATCH))
    def _(group):
        rows, products = [], []
        for step in range(BATCH):
            slot = group * BATCH + step
            alive = slot < live
            row = jnp.where(alive, coords[0, slot], ROW_BLOCKS)
            col = jnp.where(alive, coords[1, slot], 0)
            picked = scaled[pl.ds(pl.multiple_of(col * BLK, BLK), BLK), :]
            rows.append(row)
            products.append(jnp.dot(values[slot], picked, preferred_element_type=f32))
        for row, product in zip(rows, products):
            total[pl.ds(pl.multiple_of(row * BLK, BLK), BLK), :] += product

    for near in range(NEAR):
        for far in range(FAR):
            dest = far * NEAR + near
            out[near, far * OWN : (far + 1) * OWN] = total[dest * OWN : (dest + 1) * OWN].astype(bf16)
        out[near, FAR * OWN :] = row_sums[near]


def near_kernel(pieces, out):
    sums = pieces[0, FAR * OWN :].astype(f32)
    for near in range(1, NEAR):
        sums += pieces[near, FAR * OWN :].astype(f32)
    high, low = split(sums[: 2 * FAR] + sums[2 * FAR :])
    for far in range(FAR):
        rows = pieces[0, far * OWN : (far + 1) * OWN].astype(f32)
        for near in range(1, NEAR):
            rows += pieces[near, far * OWN : (far + 1) * OWN].astype(f32)
        pair = slice(2 * far, 2 * far + 2)
        tail = jnp.concatenate([high[pair], low[pair], jnp.zeros((4, BLK), f32)], axis=0)
        out[far] = jnp.concatenate([rows, tail], axis=0).astype(bf16)


def far_kernel(odd, pieces, out):
    rows = pieces[0].astype(f32)
    for far in range(1, FAR):
        rows += pieces[far].astype(f32)
    sums = rows[OWN : OWN + 8]
    degree = 1.0 + (sums[0:2] + sums[2:4])
    scale = jnp.concatenate([lax.rsqrt(degree), jnp.zeros((BLK - 2, BLK), f32)], axis=0).T
    halves = [scale[(h % 2) * HALF : (h % 2 + 1) * HALF, h // 2 : h // 2 + 1] for h in range(4)]
    for part in range(OWN // HALF):
        factor = jnp.where(odd[0] == 1, halves[part + 1], halves[part])
        piece = rows[part * HALF : (part + 1) * HALF] * factor
        out[part * HALF : (part + 1) * HALF] = jnp.maximum(piece, 0.0).astype(bf16)


def params(mebibytes=32):
    return pltpu.CompilerParams(vmem_limit_bytes=mebibytes * 1024 * 1024)


def shards(features, weight, block_values, block_coords, block_counts):
    coords = block_coords.T
    core = (lax.axis_index("row") % 2).astype(jnp.int32).reshape(1)
    odd = (lax.axis_index("col") % 2).astype(jnp.int32).reshape(1)

    outgoing = pl.pallas_call(
        column_sums_kernel,
        out_shape=jax.ShapeDtypeStruct((CHIPS, GATHER_ROWS, F), bf16),
        in_specs=[HBM, HBM, HBM, HBM],
        out_specs=VMEM,
        scratch_shapes=[
            pltpu.SMEM((1,), jnp.int32),
            pltpu.SMEM((2, SLOTS), jnp.int32),
            pltpu.VMEM((SLOTS, BLK, BLK), bf16),
            pltpu.VMEM((OWN, F), bf16),
            pltpu.VMEM((32, BLK), f32),
            pltpu.VMEM((2 * COL_BLOCKS, BLK), f32),
            pltpu.SemaphoreType.DMA((3,)),
            pltpu.SemaphoreType.DMA((SLOTS // UNROLL,)),
        ],
        compiler_params=params(60),
    )(block_counts, coords, block_values, features)
    mine = lax.all_to_all(outgoing, "row", 0, 0, axis_index_groups=CHIP_GROUPS, tiled=True)
    other = lax.ppermute(mine, "row", [(r, r ^ 1) for r in range(N_ROW)])

    row_sums = pl.pallas_call(
        row_sums_kernel,
        out_shape=jax.ShapeDtypeStruct((NEAR, 4 * FAR, BLK), bf16),
        in_specs=[HBM, SMEM, SMEM, VMEM],
        out_specs=VMEM,
        scratch_shapes=[pltpu.VMEM((BLK, BLK), f32)],
        compiler_params=params(),
        cost_estimate=pl.CostEstimate(flops=2 * SLOTS * BLK**3, bytes_accessed=2 * SLOTS * BLK**2, transcendentals=0),
    )(mine, block_counts, coords, block_values)

    partial = pl.pallas_call(
        aggregate_kernel,
        out_shape=jax.ShapeDtypeStruct((NEAR, NEAR_ROWS, F), bf16),
        in_specs=[SMEM, SMEM, SMEM, VMEM, VMEM, VMEM, VMEM, VMEM],
        out_specs=VMEM,
        scratch_shapes=[
            pltpu.VMEM((BLK, BLK), f32),
            pltpu.VMEM((COL_BLOCKS * BLK, F), bf16),
            pltpu.VMEM(((ROW_BLOCKS + 1) * BLK, F), f32),
        ],
        compiler_params=params(),
    )(core, block_counts, coords, mine, other, weight, block_values, row_sums)
    partial = lax.all_to_all(partial, "col", 0, 0, axis_index_groups=NEAR_GROUPS, tiled=True)

    reduced = pl.pallas_call(
        near_kernel,
        out_shape=jax.ShapeDtypeStruct((FAR, FAR_ROWS, F), bf16),
        in_specs=[VMEM],
        out_specs=VMEM,
        compiler_params=params(),
    )(partial)
    reduced = lax.all_to_all(reduced, "col", 0, 0, axis_index_groups=FAR_GROUPS, tiled=True)

    return pl.pallas_call(
        far_kernel,
        out_shape=jax.ShapeDtypeStruct((OWN, F), bf16),
        in_specs=[SMEM, VMEM],
        out_specs=VMEM,
        compiler_params=params(),
    )(odd, reduced)


def solution(mesh):
    return jax.shard_map(
        shards,
        mesh=mesh,
        in_specs=(
            P(("col", "row"), None),
            P(),
            P(("row", "col"), None, None),
            P(("row", "col"), None),
            P(("row", "col")),
        ),
        out_specs=P(("row", "col"), None),
        check_vma=False,
    )
```

```python
import jax
import jax.numpy as jnp
from jax import lax
from jax.experimental import pallas as pl
from jax.experimental.pallas import tpu as pltpu
from jax.sharding import PartitionSpec as P

F = 128
BLK = 128
SLOTS = 64
ROW_BLOCKS = 48
COL_BLOCKS = 24
OWN = 192
N_ROW = 16
N_COL = 32
CHIPS = N_ROW // 2
NEAR = 4
FAR = N_COL // NEAR
HALF = 64
UNROLL = 8
BATCH = 16

GATHER_ROWS = OWN + 2 * COL_BLOCKS
NEAR_ROWS = FAR * OWN + 4 * FAR
FAR_ROWS = OWN + 8

CHIP_GROUPS = [[2 * m + core for m in range(CHIPS)] for core in range(2)]


def near_groups():
    groups = []
    for row in range(N_ROW):
        for far in range(FAR):
            even = (far + row % 2) % FAR
            zs = (2 * even, 2 * far + 1)
            groups.append([row * N_COL + 2 * zs[near // 2] + near % 2 for near in range(NEAR)])
    return groups


FAR_GROUPS = [[NEAR * far + near for far in range(FAR)] for near in range(NEAR)]

VMEM = pl.BlockSpec(memory_space=pltpu.VMEM)
SMEM = pl.BlockSpec(memory_space=pltpu.SMEM)
HBM = pl.BlockSpec(memory_space=pltpu.HBM)
f32 = jnp.float32
bf16 = jnp.bfloat16


def split(value):
    high = value.astype(bf16).astype(f32)
    return high, value - high


def column_sums_kernel(counts_in, coords_in, values_in, features_in, out, counts, coords, values, features, sums, parts, small_sems, sems):
    small = [
        pltpu.make_async_copy(counts_in, counts, small_sems.at[0]),
        pltpu.make_async_copy(coords_in, coords, small_sems.at[1]),
        pltpu.make_async_copy(features_in, features, small_sems.at[2]),
    ]
    for copy in small:
        copy.start()
    chunks = []
    for group in range(SLOTS // UNROLL):
        slots = pl.ds(group * UNROLL, UNROLL)
        chunks.append(pltpu.make_async_copy(values_in.at[slots], values.at[slots], sems.at[group]))
        chunks[-1].start()
    sums[...] = jnp.zeros_like(sums)
    small[2].wait()
    for m in range(CHIPS):
        out[m, :OWN] = features[...]
    small[0].wait()
    small[1].wait()
    live = counts[0]
    for group in range(SLOTS // UNROLL):
        chunks[group].wait()

        @pl.when(group * UNROLL < live)
        def _():
            for step in range(UNROLL):
                slot = group * UNROLL + step
                col = jnp.where(slot < live, coords[1, slot], COL_BLOCKS)
                sums[pl.ds(col, 1), :] += jnp.sum(values[slot].astype(f32), axis=0, keepdims=True)

    high, low = split(sums[:COL_BLOCKS])
    parts[:COL_BLOCKS] = high
    parts[COL_BLOCKS:] = low
    for m in range(CHIPS):
        out[m, OWN:] = parts[...].astype(bf16)


def row_sums_kernel(mine, counts, coords, values, out, sums):
    live = counts[0]
    sums[...] = jnp.zeros_like(sums)
    lane = lax.broadcasted_iota(jnp.int32, (BLK, BLK), 1)

    @pl.loop(0, lax.div(live + BATCH - 1, BATCH))
    def _(group):
        added = sums[...]
        for step in range(BATCH):
            slot = group * BATCH + step
            row = jnp.where(slot < live, coords[0, slot], ROW_BLOCKS)
            picked = (lane == row).astype(f32).astype(bf16)
            added += jnp.dot(values[slot], picked, preferred_element_type=f32)
        sums[...] = added

    high, low = split(sums[...].T)
    for near in range(NEAR):
        picks = []
        for part in (high, low):
            for far in range(FAR):
                first = (far * NEAR + near) * OWN // BLK
                picks.append(part[first : first + 2])
        out[near] = jnp.concatenate(picks, axis=0).astype(bf16)


def aggregate_kernel(core, counts, coords, mine, other, weight, values, row_sums, out, scales, scaled, total):
    live = counts[0]
    sums = jnp.zeros((2 * COL_BLOCKS, BLK), f32)
    for m in range(CHIPS):
        sums += mine[m, OWN:].astype(f32) + other[m, OWN:].astype(f32)
    degree = 1.0 + (sums[:COL_BLOCKS] + sums[COL_BLOCKS:])
    scales[...] = jnp.zeros_like(scales)
    scales[:COL_BLOCKS] = lax.rsqrt(degree)
    scales[...] = scales[...].T

    def scale(pieces):
        for r in range(N_ROW):
            transformed = jnp.dot(pieces[r % 2][r // 2, :OWN], weight[...], preferred_element_type=f32)
            for part in range(OWN // HALF):
                h = r * (OWN // HALF) + part
                factor = scales[(h % 2) * HALF : (h % 2 + 1) * HALF, h // 2 : h // 2 + 1]
                rows = transformed[part * HALF : (part + 1) * HALF]
                scaled[h * HALF : (h + 1) * HALF] = (rows * factor).astype(bf16)

    @pl.when(core[0] == 0)
    def _():
        scale((mine, other))

    @pl.when(core[0] == 1)
    def _():
        scale((other, mine))

    total[...] = jnp.zeros_like(total)

    @pl.loop(0, lax.div(live + BATCH - 1, BATCH))
    def _(group):
        rows, products = [], []
        for step in range(BATCH):
            slot = group * BATCH + step
            alive = slot < live
            row = jnp.where(alive, coords[0, slot], ROW_BLOCKS)
            col = jnp.where(alive, coords[1, slot], 0)
            picked = scaled[pl.ds(pl.multiple_of(col * BLK, BLK), BLK), :]
            rows.append(row)
            products.append(jnp.dot(values[slot], picked, preferred_element_type=f32))
        for row, product in zip(rows, products):
            total[pl.ds(pl.multiple_of(row * BLK, BLK), BLK), :] += product

    for near in range(NEAR):
        for far in range(FAR):
            dest = far * NEAR + near
            out[near, far * OWN : (far + 1) * OWN] = total[dest * OWN : (dest + 1) * OWN].astype(bf16)
        out[near, FAR * OWN :] = row_sums[near]


def near_kernel(pieces, out):
    sums = pieces[0, FAR * OWN :].astype(f32)
    for near in range(1, NEAR):
        sums += pieces[near, FAR * OWN :].astype(f32)
    high, low = split(sums[: 2 * FAR] + sums[2 * FAR :])
    for far in range(FAR):
        rows = pieces[0, far * OWN : (far + 1) * OWN].astype(f32)
        for near in range(1, NEAR):
            rows += pieces[near, far * OWN : (far + 1) * OWN].astype(f32)
        pair = slice(2 * far, 2 * far + 2)
        tail = jnp.concatenate([high[pair], low[pair], jnp.zeros((4, BLK), f32)], axis=0)
        out[far] = jnp.concatenate([rows, tail], axis=0).astype(bf16)


def far_kernel(odd, pieces, out):
    rows = pieces[0].astype(f32)
    for far in range(1, FAR):
        rows += pieces[far].astype(f32)
    sums = rows[OWN : OWN + 8]
    degree = 1.0 + (sums[0:2] + sums[2:4])
    scale = jnp.concatenate([lax.rsqrt(degree), jnp.zeros((BLK - 2, BLK), f32)], axis=0).T
    halves = [scale[(h % 2) * HALF : (h % 2 + 1) * HALF, h // 2 : h // 2 + 1] for h in range(4)]
    for part in range(OWN // HALF):
        factor = jnp.where(odd[0] == 1, halves[part + 1], halves[part])
        piece = rows[part * HALF : (part + 1) * HALF] * factor
        out[part * HALF : (part + 1) * HALF] = jnp.maximum(piece, 0.0).astype(bf16)


def params(mebibytes=32):
    return pltpu.CompilerParams(vmem_limit_bytes=mebibytes * 1024 * 1024)


def shards(features, weight, block_values, block_coords, block_counts):
    coords = block_coords.T
    core = (lax.axis_index("row") % 2).astype(jnp.int32).reshape(1)
    odd = (lax.axis_index("col") % 2).astype(jnp.int32).reshape(1)

    outgoing = pl.pallas_call(
        column_sums_kernel,
        out_shape=jax.ShapeDtypeStruct((CHIPS, GATHER_ROWS, F), bf16),
        in_specs=[HBM, HBM, HBM, HBM],
        out_specs=VMEM,
        scratch_shapes=[
            pltpu.SMEM((1,), jnp.int32),
            pltpu.SMEM((2, SLOTS), jnp.int32),
            pltpu.VMEM((SLOTS, BLK, BLK), bf16),
            pltpu.VMEM((OWN, F), bf16),
            pltpu.VMEM((32, BLK), f32),
            pltpu.VMEM((2 * COL_BLOCKS, BLK), f32),
            pltpu.SemaphoreType.DMA((3,)),
            pltpu.SemaphoreType.DMA((SLOTS // UNROLL,)),
        ],
        compiler_params=params(60),
    )(block_counts, coords, block_values, features)
    mine = lax.all_to_all(outgoing, "row", 0, 0, axis_index_groups=CHIP_GROUPS, tiled=True)
    other = lax.ppermute(mine, "row", [(r, r ^ 1) for r in range(N_ROW)])

    row_sums = pl.pallas_call(
        row_sums_kernel,
        out_shape=jax.ShapeDtypeStruct((NEAR, 4 * FAR, BLK), bf16),
        in_specs=[HBM, SMEM, SMEM, VMEM],
        out_specs=VMEM,
        scratch_shapes=[pltpu.VMEM((BLK, BLK), f32)],
        compiler_params=params(),
        cost_estimate=pl.CostEstimate(flops=2 * SLOTS * BLK**3, bytes_accessed=2 * SLOTS * BLK**2, transcendentals=0),
    )(mine, block_counts, coords, block_values)

    partial = pl.pallas_call(
        aggregate_kernel,
        out_shape=jax.ShapeDtypeStruct((NEAR, NEAR_ROWS, F), bf16),
        in_specs=[SMEM, SMEM, SMEM, VMEM, VMEM, VMEM, VMEM, VMEM],
        out_specs=VMEM,
        scratch_shapes=[
            pltpu.VMEM((BLK, BLK), f32),
            pltpu.VMEM((COL_BLOCKS * BLK, F), bf16),
            pltpu.VMEM(((ROW_BLOCKS + 1) * BLK, F), f32),
        ],
        compiler_params=params(),
    )(core, block_counts, coords, mine, other, weight, block_values, row_sums)
    partial = lax.all_to_all(partial, ("row", "col"), 0, 0, axis_index_groups=near_groups(), tiled=True)

    reduced = pl.pallas_call(
        near_kernel,
        out_shape=jax.ShapeDtypeStruct((FAR, FAR_ROWS, F), bf16),
        in_specs=[VMEM],
        out_specs=VMEM,
        compiler_params=params(),
    )(partial)
    reduced = lax.all_to_all(reduced, "col", 0, 0, axis_index_groups=FAR_GROUPS, tiled=True)

    return pl.pallas_call(
        far_kernel,
        out_shape=jax.ShapeDtypeStruct((OWN, F), bf16),
        in_specs=[SMEM, VMEM],
        out_specs=VMEM,
        compiler_params=params(),
    )(odd, reduced)


def solution(mesh):
    return jax.shard_map(
        shards,
        mesh=mesh,
        in_specs=(
            P(("col", "row"), None),
            P(),
            P(("row", "col"), None, None),
            P(("row", "col"), None),
            P(("row", "col")),
        ),
        out_specs=P(("row", "col"), None),
        check_vma=False,
    )
```

```python
import jax
import jax.numpy as jnp
from jax import lax
from jax.experimental import pallas as pl
from jax.experimental.pallas import tpu as pltpu
from jax.sharding import PartitionSpec as P

F = 128
BLK = 128
SLOTS = 64
ROW_BLOCKS = 48
COL_BLOCKS = 24
OWN = 192
N_ROW = 16
N_COL = 32
CHIPS = N_ROW // 2
NEAR = 4
FAR = N_COL // NEAR
HALF = 64
UNROLL = 8
BATCH = 32

GATHER_ROWS = OWN + COL_BLOCKS
NEAR_ROWS = FAR * OWN + 4 * FAR
FAR_ROWS = OWN + 8

CHIP_GROUPS = [[2 * m + core for m in range(CHIPS)] for core in range(2)]


def near_groups():
    groups = []
    for row in range(N_ROW):
        for far in range(FAR):
            even = (far + row % 2) % FAR
            zs = (2 * even, 2 * far + 1)
            groups.append([row * N_COL + 2 * zs[near // 2] + near % 2 for near in range(NEAR)])
    return groups


FAR_GROUPS = [[NEAR * far + near for far in range(FAR)] for near in range(NEAR)]

VMEM = pl.BlockSpec(memory_space=pltpu.VMEM)
SMEM = pl.BlockSpec(memory_space=pltpu.SMEM)
HBM = pl.BlockSpec(memory_space=pltpu.HBM)
f32 = jnp.float32
bf16 = jnp.bfloat16


def split(value):
    high = value.astype(bf16).astype(f32)
    return high, value - high


def column_sums_kernel(counts_in, coords_in, values_in, features_in, out, counts, coords, values, features, sums, small_sems, sems):
    small = [
        pltpu.make_async_copy(counts_in, counts, small_sems.at[0]),
        pltpu.make_async_copy(coords_in, coords, small_sems.at[1]),
        pltpu.make_async_copy(features_in, features, small_sems.at[2]),
    ]
    for copy in small:
        copy.start()
    chunks = []
    for group in range(SLOTS // UNROLL):
        slots = pl.ds(group * UNROLL, UNROLL)
        chunks.append(pltpu.make_async_copy(values_in.at[slots], values.at[slots], sems.at[group]))
        chunks[-1].start()
    sums[...] = jnp.zeros_like(sums)
    small[2].wait()
    for m in range(CHIPS):
        out[m, :OWN] = features[...]
    small[0].wait()
    small[1].wait()
    live = counts[0]
    for group in range(SLOTS // UNROLL):
        chunks[group].wait()

        @pl.when(group * UNROLL < live)
        def _():
            for step in range(UNROLL):
                slot = group * UNROLL + step
                col = jnp.where(slot < live, coords[1, slot], COL_BLOCKS)
                sums[pl.ds(col, 1), :] += jnp.sum(values[slot].astype(f32), axis=0, keepdims=True)

    for m in range(CHIPS):
        out[m, OWN:] = sums[:COL_BLOCKS].astype(bf16)


def row_sums_kernel(mine, counts, coords, values, out, sums):
    live = counts[0]
    sums[...] = jnp.zeros_like(sums)
    lane = lax.broadcasted_iota(jnp.int32, (BLK, BLK), 1)

    @pl.loop(0, lax.div(live + BATCH - 1, BATCH))
    def _(group):
        added = sums[...]
        for step in range(BATCH):
            slot = group * BATCH + step
            row = jnp.where(slot < live, coords[0, slot], ROW_BLOCKS)
            picked = (lane == row).astype(f32).astype(bf16)
            added += jnp.dot(values[slot], picked, preferred_element_type=f32)
        sums[...] = added

    high, low = split(sums[...].T)
    for near in range(NEAR):
        picks = []
        for part in (high, low):
            for far in range(FAR):
                first = (far * NEAR + near) * OWN // BLK
                picks.append(part[first : first + 2])
        out[near] = jnp.concatenate(picks, axis=0).astype(bf16)


def aggregate_kernel(core, counts, coords, mine, other, weight, values, row_sums, out, scales, scaled, total):
    live = counts[0]
    sums = jnp.zeros((COL_BLOCKS, BLK), f32)
    for m in range(CHIPS):
        sums += mine[m, OWN:].astype(f32) + other[m, OWN:].astype(f32)
    degree = 1.0 + sums
    scales[...] = jnp.zeros_like(scales)
    scales[:COL_BLOCKS] = lax.rsqrt(degree)
    scales[...] = scales[...].T

    def scale(pieces):
        for r in range(N_ROW):
            transformed = jnp.dot(pieces[r % 2][r // 2, :OWN], weight[...], preferred_element_type=f32)
            for part in range(OWN // HALF):
                h = r * (OWN // HALF) + part
                factor = scales[(h % 2) * HALF : (h % 2 + 1) * HALF, h // 2 : h // 2 + 1]
                rows = transformed[part * HALF : (part + 1) * HALF]
                scaled[h * HALF : (h + 1) * HALF] = (rows * factor).astype(bf16)

    @pl.when(core[0] == 0)
    def _():
        scale((mine, other))

    @pl.when(core[0] == 1)
    def _():
        scale((other, mine))

    total[...] = jnp.zeros_like(total)

    @pl.loop(0, lax.div(live + BATCH - 1, BATCH))
    def _(group):
        rows, products = [], []
        for step in range(BATCH):
            slot = group * BATCH + step
            alive = slot < live
            row = jnp.where(alive, coords[0, slot], ROW_BLOCKS)
            col = jnp.where(alive, coords[1, slot], 0)
            picked = scaled[pl.ds(pl.multiple_of(col * BLK, BLK), BLK), :]
            rows.append(row)
            products.append(jnp.dot(values[slot], picked, preferred_element_type=f32))
        for row, product in zip(rows, products):
            total[pl.ds(pl.multiple_of(row * BLK, BLK), BLK), :] += product

    for near in range(NEAR):
        for far in range(FAR):
            dest = far * NEAR + near
            out[near, far * OWN : (far + 1) * OWN] = total[dest * OWN : (dest + 1) * OWN].astype(bf16)
        out[near, FAR * OWN :] = row_sums[near]


def near_kernel(pieces, out):
    sums = pieces[0, FAR * OWN :].astype(f32)
    for near in range(1, NEAR):
        sums += pieces[near, FAR * OWN :].astype(f32)
    high, low = split(sums[: 2 * FAR] + sums[2 * FAR :])
    for far in range(FAR):
        rows = pieces[0, far * OWN : (far + 1) * OWN].astype(f32)
        for near in range(1, NEAR):
            rows += pieces[near, far * OWN : (far + 1) * OWN].astype(f32)
        pair = slice(2 * far, 2 * far + 2)
        tail = jnp.concatenate([high[pair], low[pair], jnp.zeros((4, BLK), f32)], axis=0)
        out[far] = jnp.concatenate([rows, tail], axis=0).astype(bf16)


def far_kernel(odd, pieces, out):
    rows = pieces[0].astype(f32)
    for far in range(1, FAR):
        rows += pieces[far].astype(f32)
    sums = rows[OWN : OWN + 8]
    degree = 1.0 + (sums[0:2] + sums[2:4])
    scale = jnp.concatenate([lax.rsqrt(degree), jnp.zeros((BLK - 2, BLK), f32)], axis=0).T
    halves = [scale[(h % 2) * HALF : (h % 2 + 1) * HALF, h // 2 : h // 2 + 1] for h in range(4)]
    for part in range(OWN // HALF):
        factor = jnp.where(odd[0] == 1, halves[part + 1], halves[part])
        piece = rows[part * HALF : (part + 1) * HALF] * factor
        out[part * HALF : (part + 1) * HALF] = jnp.maximum(piece, 0.0).astype(bf16)


def params(mebibytes=32):
    return pltpu.CompilerParams(vmem_limit_bytes=mebibytes * 1024 * 1024)


def shards(features, weight, block_values, block_coords, block_counts):
    coords = block_coords.T
    core = (lax.axis_index("row") % 2).astype(jnp.int32).reshape(1)
    odd = (lax.axis_index("col") % 2).astype(jnp.int32).reshape(1)

    outgoing = pl.pallas_call(
        column_sums_kernel,
        out_shape=jax.ShapeDtypeStruct((CHIPS, GATHER_ROWS, F), bf16),
        in_specs=[HBM, HBM, HBM, HBM],
        out_specs=VMEM,
        scratch_shapes=[
            pltpu.SMEM((1,), jnp.int32),
            pltpu.SMEM((2, SLOTS), jnp.int32),
            pltpu.VMEM((SLOTS, BLK, BLK), bf16),
            pltpu.VMEM((OWN, F), bf16),
            pltpu.VMEM((32, BLK), f32),
            pltpu.SemaphoreType.DMA((3,)),
            pltpu.SemaphoreType.DMA((SLOTS // UNROLL,)),
        ],
        compiler_params=params(60),
    )(block_counts, coords, block_values, features)
    mine = lax.all_to_all(outgoing, "row", 0, 0, axis_index_groups=CHIP_GROUPS, tiled=True)
    other = lax.ppermute(mine, "row", [(r, r ^ 1) for r in range(N_ROW)])

    row_sums = pl.pallas_call(
        row_sums_kernel,
        out_shape=jax.ShapeDtypeStruct((NEAR, 4 * FAR, BLK), bf16),
        in_specs=[HBM, SMEM, SMEM, VMEM],
        out_specs=VMEM,
        scratch_shapes=[pltpu.VMEM((BLK, BLK), f32)],
        compiler_params=params(),
        cost_estimate=pl.CostEstimate(flops=2 * SLOTS * BLK**3, bytes_accessed=2 * SLOTS * BLK**2, transcendentals=0),
    )(mine, block_counts, coords, block_values)

    partial = pl.pallas_call(
        aggregate_kernel,
        out_shape=jax.ShapeDtypeStruct((NEAR, NEAR_ROWS, F), bf16),
        in_specs=[SMEM, SMEM, SMEM, VMEM, VMEM, VMEM, VMEM, VMEM],
        out_specs=VMEM,
        scratch_shapes=[
            pltpu.VMEM((BLK, BLK), f32),
            pltpu.VMEM((COL_BLOCKS * BLK, F), bf16),
            pltpu.VMEM(((ROW_BLOCKS + 1) * BLK, F), f32),
        ],
        compiler_params=params(),
    )(core, block_counts, coords, mine, other, weight, block_values, row_sums)
    partial = lax.all_to_all(partial, ("row", "col"), 0, 0, axis_index_groups=near_groups(), tiled=True)

    reduced = pl.pallas_call(
        near_kernel,
        out_shape=jax.ShapeDtypeStruct((FAR, FAR_ROWS, F), bf16),
        in_specs=[VMEM],
        out_specs=VMEM,
        compiler_params=params(),
    )(partial)
    reduced = lax.all_to_all(reduced, "col", 0, 0, axis_index_groups=FAR_GROUPS, tiled=True)

    return pl.pallas_call(
        far_kernel,
        out_shape=jax.ShapeDtypeStruct((OWN, F), bf16),
        in_specs=[SMEM, VMEM],
        out_specs=VMEM,
        compiler_params=params(),
    )(odd, reduced)


def solution(mesh):
    return jax.shard_map(
        shards,
        mesh=mesh,
        in_specs=(
            P(("col", "row"), None),
            P(),
            P(("row", "col"), None, None),
            P(("row", "col"), None),
            P(("row", "col")),
        ),
        out_specs=P(("row", "col"), None),
        check_vma=False,
    )
```

```python
import jax
import jax.numpy as jnp
from jax import lax
from jax.experimental import pallas as pl
from jax.experimental.pallas import tpu as pltpu
from jax.sharding import PartitionSpec as P

F = 128
BLK = 128
SLOTS = 64
ROW_BLOCKS = 48
COL_BLOCKS = 24
OWN = 192
N_ROW = 16
N_COL = 32
CHIPS = N_ROW // 2
NEAR = 4
FAR = N_COL // NEAR
HALF = 64
UNROLL = 8
BATCH = 32

GATHER_ROWS = OWN + COL_BLOCKS
NEAR_ROWS = FAR * OWN + 4 * FAR
FAR_ROWS = OWN + 8

CHIP_TURN = 5
FAR_TURN = 4


def owner(near, far):
    return NEAR * ((far + FAR_TURN) % FAR) + near


CHIP_GROUPS = [[2 * ((m + CHIP_TURN) % CHIPS) + core for m in range(CHIPS)] for core in range(2)]


def near_groups():
    groups = []
    for row in range(N_ROW):
        for far in range(FAR):
            even = (far + row % 2) % FAR
            zs = (2 * even, 2 * far + 1)
            groups.append([row * N_COL + 2 * zs[near // 2] + near % 2 for near in range(NEAR)])
    return groups


FAR_GROUPS = [[owner(near, far) for far in range(FAR)] for near in range(NEAR)]

VMEM = pl.BlockSpec(memory_space=pltpu.VMEM)
SMEM = pl.BlockSpec(memory_space=pltpu.SMEM)
HBM = pl.BlockSpec(memory_space=pltpu.HBM)
f32 = jnp.float32
bf16 = jnp.bfloat16


def split(value):
    high = value.astype(bf16).astype(f32)
    return high, value - high


def column_sums_kernel(counts_in, coords_in, values_in, features_in, out, counts, coords, values, features, sums, small_sems, sems):
    small = [
        pltpu.make_async_copy(counts_in, counts, small_sems.at[0]),
        pltpu.make_async_copy(coords_in, coords, small_sems.at[1]),
        pltpu.make_async_copy(features_in, features, small_sems.at[2]),
    ]
    for copy in small:
        copy.start()
    chunks = []
    for group in range(SLOTS // UNROLL):
        slots = pl.ds(group * UNROLL, UNROLL)
        chunks.append(pltpu.make_async_copy(values_in.at[slots], values.at[slots], sems.at[group]))
        chunks[-1].start()
    sums[...] = jnp.zeros_like(sums)
    small[2].wait()
    for m in range(CHIPS):
        out[m, :OWN] = features[...]
    small[0].wait()
    small[1].wait()
    live = counts[0]
    for group in range(SLOTS // UNROLL):
        chunks[group].wait()

        @pl.when(group * UNROLL < live)
        def _():
            for step in range(UNROLL):
                slot = group * UNROLL + step
                col = jnp.where(slot < live, coords[1, slot], COL_BLOCKS)
                sums[pl.ds(col, 1), :] += jnp.sum(values[slot].astype(f32), axis=0, keepdims=True)

    for m in range(CHIPS):
        out[m, OWN:] = sums[:COL_BLOCKS].astype(bf16)


def row_sums_kernel(mine, counts, coords, values, out, sums):
    live = counts[0]
    sums[...] = jnp.zeros_like(sums)
    lane = lax.broadcasted_iota(jnp.int32, (BLK, BLK), 1)

    @pl.loop(0, lax.div(live + BATCH - 1, BATCH))
    def _(group):
        added = sums[...]
        for step in range(BATCH):
            slot = group * BATCH + step
            row = jnp.where(slot < live, coords[0, slot], ROW_BLOCKS)
            picked = (lane == row).astype(f32).astype(bf16)
            added += jnp.dot(values[slot], picked, preferred_element_type=f32)
        sums[...] = added

    high, low = split(sums[...].T)
    for near in range(NEAR):
        picks = []
        for part in (high, low):
            for far in range(FAR):
                first = owner(near, far) * OWN // BLK
                picks.append(part[first : first + 2])
        out[near] = jnp.concatenate(picks, axis=0).astype(bf16)


def aggregate_kernel(core, counts, coords, mine, other, weight, values, row_sums, out, scales, scaled, total):
    live = counts[0]
    sums = jnp.zeros((COL_BLOCKS, BLK), f32)
    for m in range(CHIPS):
        sums += mine[m, OWN:].astype(f32) + other[m, OWN:].astype(f32)
    degree = 1.0 + sums
    scales[...] = jnp.zeros_like(scales)
    scales[:COL_BLOCKS] = lax.rsqrt(degree)
    scales[...] = scales[...].T

    def scale(pieces):
        for r in range(N_ROW):
            transformed = jnp.dot(pieces[r % 2][(r // 2 - CHIP_TURN) % CHIPS, :OWN], weight[...], preferred_element_type=f32)
            for part in range(OWN // HALF):
                h = r * (OWN // HALF) + part
                factor = scales[(h % 2) * HALF : (h % 2 + 1) * HALF, h // 2 : h // 2 + 1]
                rows = transformed[part * HALF : (part + 1) * HALF]
                scaled[h * HALF : (h + 1) * HALF] = (rows * factor).astype(bf16)

    @pl.when(core[0] == 0)
    def _():
        scale((mine, other))

    @pl.when(core[0] == 1)
    def _():
        scale((other, mine))

    total[...] = jnp.zeros_like(total)

    @pl.loop(0, lax.div(live + BATCH - 1, BATCH))
    def _(group):
        rows, products = [], []
        for step in range(BATCH):
            slot = group * BATCH + step
            alive = slot < live
            row = jnp.where(alive, coords[0, slot], ROW_BLOCKS)
            col = jnp.where(alive, coords[1, slot], 0)
            picked = scaled[pl.ds(pl.multiple_of(col * BLK, BLK), BLK), :]
            rows.append(row)
            products.append(jnp.dot(values[slot], picked, preferred_element_type=f32))
        for row, product in zip(rows, products):
            total[pl.ds(pl.multiple_of(row * BLK, BLK), BLK), :] += product

    for near in range(NEAR):
        for far in range(FAR):
            dest = owner(near, far)
            out[near, far * OWN : (far + 1) * OWN] = total[dest * OWN : (dest + 1) * OWN].astype(bf16)
        out[near, FAR * OWN :] = row_sums[near]


def near_kernel(pieces, out):
    sums = pieces[0, FAR * OWN :].astype(f32)
    for near in range(1, NEAR):
        sums += pieces[near, FAR * OWN :].astype(f32)
    high, low = split(sums[: 2 * FAR] + sums[2 * FAR :])
    for far in range(FAR):
        rows = pieces[0, far * OWN : (far + 1) * OWN].astype(f32)
        for near in range(1, NEAR):
            rows += pieces[near, far * OWN : (far + 1) * OWN].astype(f32)
        pair = slice(2 * far, 2 * far + 2)
        tail = jnp.concatenate([high[pair], low[pair], jnp.zeros((4, BLK), f32)], axis=0)
        out[far] = jnp.concatenate([rows, tail], axis=0).astype(bf16)


def far_kernel(odd, pieces, out):
    rows = pieces[0].astype(f32)
    for far in range(1, FAR):
        rows += pieces[far].astype(f32)
    sums = rows[OWN : OWN + 8]
    degree = 1.0 + (sums[0:2] + sums[2:4])
    scale = jnp.concatenate([lax.rsqrt(degree), jnp.zeros((BLK - 2, BLK), f32)], axis=0).T
    halves = [scale[(h % 2) * HALF : (h % 2 + 1) * HALF, h // 2 : h // 2 + 1] for h in range(4)]
    for part in range(OWN // HALF):
        factor = jnp.where(odd[0] == 1, halves[part + 1], halves[part])
        piece = rows[part * HALF : (part + 1) * HALF] * factor
        out[part * HALF : (part + 1) * HALF] = jnp.maximum(piece, 0.0).astype(bf16)


def params(mebibytes=32):
    return pltpu.CompilerParams(vmem_limit_bytes=mebibytes * 1024 * 1024)


def shards(features, weight, block_values, block_coords, block_counts):
    coords = block_coords.T
    core = (lax.axis_index("row") % 2).astype(jnp.int32).reshape(1)
    odd = (lax.axis_index("col") % 2).astype(jnp.int32).reshape(1)

    outgoing = pl.pallas_call(
        column_sums_kernel,
        out_shape=jax.ShapeDtypeStruct((CHIPS, GATHER_ROWS, F), bf16),
        in_specs=[HBM, HBM, HBM, HBM],
        out_specs=VMEM,
        scratch_shapes=[
            pltpu.SMEM((1,), jnp.int32),
            pltpu.SMEM((2, SLOTS), jnp.int32),
            pltpu.VMEM((SLOTS, BLK, BLK), bf16),
            pltpu.VMEM((OWN, F), bf16),
            pltpu.VMEM((32, BLK), f32),
            pltpu.SemaphoreType.DMA((3,)),
            pltpu.SemaphoreType.DMA((SLOTS // UNROLL,)),
        ],
        compiler_params=params(60),
    )(block_counts, coords, block_values, features)
    mine = lax.all_to_all(outgoing, "row", 0, 0, axis_index_groups=CHIP_GROUPS, tiled=True)
    other = lax.ppermute(mine, "row", [(r, r ^ 1) for r in range(N_ROW)])

    row_sums = pl.pallas_call(
        row_sums_kernel,
        out_shape=jax.ShapeDtypeStruct((NEAR, 4 * FAR, BLK), bf16),
        in_specs=[HBM, SMEM, SMEM, VMEM],
        out_specs=VMEM,
        scratch_shapes=[pltpu.VMEM((BLK, BLK), f32)],
        compiler_params=params(),
        cost_estimate=pl.CostEstimate(flops=2 * SLOTS * BLK**3, bytes_accessed=2 * SLOTS * BLK**2, transcendentals=0),
    )(mine, block_counts, coords, block_values)

    partial = pl.pallas_call(
        aggregate_kernel,
        out_shape=jax.ShapeDtypeStruct((NEAR, NEAR_ROWS, F), bf16),
        in_specs=[SMEM, SMEM, SMEM, VMEM, VMEM, VMEM, VMEM, VMEM],
        out_specs=VMEM,
        scratch_shapes=[
            pltpu.VMEM((BLK, BLK), f32),
            pltpu.VMEM((COL_BLOCKS * BLK, F), bf16),
            pltpu.VMEM(((ROW_BLOCKS + 1) * BLK, F), f32),
        ],
        compiler_params=params(),
    )(core, block_counts, coords, mine, other, weight, block_values, row_sums)
    partial = lax.all_to_all(partial, ("row", "col"), 0, 0, axis_index_groups=near_groups(), tiled=True)

    reduced = pl.pallas_call(
        near_kernel,
        out_shape=jax.ShapeDtypeStruct((FAR, FAR_ROWS, F), bf16),
        in_specs=[VMEM],
        out_specs=VMEM,
        compiler_params=params(),
    )(partial)
    reduced = lax.all_to_all(reduced, "col", 0, 0, axis_index_groups=FAR_GROUPS, tiled=True)

    return pl.pallas_call(
        far_kernel,
        out_shape=jax.ShapeDtypeStruct((OWN, F), bf16),
        in_specs=[SMEM, VMEM],
        out_specs=VMEM,
        compiler_params=params(),
    )(odd, reduced)


def solution(mesh):
    return jax.shard_map(
        shards,
        mesh=mesh,
        in_specs=(
            P(("col", "row"), None),
            P(),
            P(("row", "col"), None, None),
            P(("row", "col"), None),
            P(("row", "col")),
        ),
        out_specs=P(("row", "col"), None),
        check_vma=False,
    )
```

```python
import jax
import jax.numpy as jnp
from jax import lax
from jax.experimental import pallas as pl
from jax.experimental.pallas import tpu as pltpu
from jax.sharding import PartitionSpec as P

F = 128
BLK = 128
SLOTS = 64
ROW_BLOCKS = 48
COL_BLOCKS = 24
OWN = 192
N_ROW = 16
N_COL = 32
CHIPS = N_ROW // 2
NEAR = 4
FAR = N_COL // NEAR
HALF = 64
UNROLL = 8
BATCH = 32

GATHER_ROWS = OWN + COL_BLOCKS
NEAR_ROWS = FAR * OWN + 4 * FAR
FAR_ROWS = OWN + 8

CHIP_TURN = 7
FAR_TURN = 5


def owner(near, far):
    return NEAR * ((far + FAR_TURN) % FAR) + near


CHIP_GROUPS = [[2 * ((m + CHIP_TURN) % CHIPS) + core for m in range(CHIPS)] for core in range(2)]


def near_groups():
    groups = []
    for row in range(N_ROW):
        for far in range(FAR):
            even = (far + row % 2) % FAR
            zs = (2 * even, 2 * far + 1)
            groups.append([row * N_COL + 2 * zs[near // 2] + near % 2 for near in range(NEAR)])
    return groups


FAR_GROUPS = [[owner(near, far) for far in range(FAR)] for near in range(NEAR)]

VMEM = pl.BlockSpec(memory_space=pltpu.VMEM)
SMEM = pl.BlockSpec(memory_space=pltpu.SMEM)
HBM = pl.BlockSpec(memory_space=pltpu.HBM)
f32 = jnp.float32
bf16 = jnp.bfloat16


def split(value):
    high = value.astype(bf16).astype(f32)
    return high, value - high


def column_sums_kernel(counts_in, coords_in, values_in, features_in, out, counts, coords, values, features, sums, small_sems, sems):
    small = [
        pltpu.make_async_copy(counts_in, counts, small_sems.at[0]),
        pltpu.make_async_copy(coords_in, coords, small_sems.at[1]),
        pltpu.make_async_copy(features_in, features, small_sems.at[2]),
    ]
    for copy in small:
        copy.start()
    chunks = []
    for group in range(SLOTS // UNROLL):
        slots = pl.ds(group * UNROLL, UNROLL)
        chunks.append(pltpu.make_async_copy(values_in.at[slots], values.at[slots], sems.at[group]))
        chunks[-1].start()
    sums[...] = jnp.zeros_like(sums)
    small[2].wait()
    for m in range(CHIPS):
        out[m, :OWN] = features[...]
    small[0].wait()
    small[1].wait()
    live = counts[0]
    for group in range(SLOTS // UNROLL):
        chunks[group].wait()

        @pl.when(group * UNROLL < live)
        def _():
            for step in range(UNROLL):
                slot = group * UNROLL + step
                col = jnp.where(slot < live, coords[1, slot], COL_BLOCKS)
                sums[pl.ds(col, 1), :] += jnp.sum(values[slot].astype(f32), axis=0, keepdims=True)

    for m in range(CHIPS):
        out[m, OWN:] = sums[:COL_BLOCKS].astype(bf16)


def row_sums_kernel(mine, counts, coords, values, out, sums):
    live = counts[0]
    sums[...] = jnp.zeros_like(sums)
    lane = lax.broadcasted_iota(jnp.int32, (BLK, BLK), 1)

    @pl.loop(0, lax.div(live + BATCH - 1, BATCH))
    def _(group):
        added = sums[...]
        for step in range(BATCH):
            slot = group * BATCH + step
            row = jnp.where(slot < live, coords[0, slot], ROW_BLOCKS)
            picked = (lane == row).astype(f32).astype(bf16)
            added += jnp.dot(values[slot], picked, preferred_element_type=f32)
        sums[...] = added

    high, low = split(sums[...].T)
    for near in range(NEAR):
        picks = []
        for part in (high, low):
            for far in range(FAR):
                first = owner(near, far) * OWN // BLK
                picks.append(part[first : first + 2])
        out[near] = jnp.concatenate(picks, axis=0).astype(bf16)


def aggregate_kernel(core, counts, coords, mine, other, weight, values, row_sums, out, scales, scaled, total):
    live = counts[0]
    sums = jnp.zeros((COL_BLOCKS, BLK), f32)
    for m in range(CHIPS):
        sums += mine[m, OWN:].astype(f32) + other[m, OWN:].astype(f32)
    degree = 1.0 + sums
    scales[...] = jnp.zeros_like(scales)
    scales[:COL_BLOCKS] = lax.rsqrt(degree)
    scales[...] = scales[...].T

    def scale(pieces):
        for r in range(N_ROW):
            transformed = jnp.dot(pieces[r % 2][(r // 2 - CHIP_TURN) % CHIPS, :OWN], weight[...], preferred_element_type=f32)
            for part in range(OWN // HALF):
                h = r * (OWN // HALF) + part
                factor = scales[(h % 2) * HALF : (h % 2 + 1) * HALF, h // 2 : h // 2 + 1]
                rows = transformed[part * HALF : (part + 1) * HALF]
                scaled[h * HALF : (h + 1) * HALF] = (rows * factor).astype(bf16)

    @pl.when(core[0] == 0)
    def _():
        scale((mine, other))

    @pl.when(core[0] == 1)
    def _():
        scale((other, mine))

    total[...] = jnp.zeros_like(total)

    @pl.loop(0, lax.div(live + BATCH - 1, BATCH))
    def _(group):
        rows, products = [], []
        for step in range(BATCH):
            slot = group * BATCH + step
            alive = slot < live
            row = jnp.where(alive, coords[0, slot], ROW_BLOCKS)
            col = jnp.where(alive, coords[1, slot], 0)
            picked = scaled[pl.ds(pl.multiple_of(col * BLK, BLK), BLK), :]
            rows.append(row)
            products.append(jnp.dot(values[slot], picked, preferred_element_type=f32))
        for row, product in zip(rows, products):
            total[pl.ds(pl.multiple_of(row * BLK, BLK), BLK), :] += product

    for near in range(NEAR):
        for far in range(FAR):
            dest = owner(near, far)
            out[near, far * OWN : (far + 1) * OWN] = total[dest * OWN : (dest + 1) * OWN].astype(bf16)
        out[near, FAR * OWN :] = row_sums[near]


def near_kernel(pieces, out):
    sums = pieces[0, FAR * OWN :].astype(f32)
    for near in range(1, NEAR):
        sums += pieces[near, FAR * OWN :].astype(f32)
    high, low = split(sums[: 2 * FAR] + sums[2 * FAR :])
    for far in range(FAR):
        rows = pieces[0, far * OWN : (far + 1) * OWN].astype(f32)
        for near in range(1, NEAR):
            rows += pieces[near, far * OWN : (far + 1) * OWN].astype(f32)
        pair = slice(2 * far, 2 * far + 2)
        tail = jnp.concatenate([high[pair], low[pair], jnp.zeros((4, BLK), f32)], axis=0)
        out[far] = jnp.concatenate([rows, tail], axis=0).astype(bf16)


def far_kernel(odd, pieces, out):
    rows = pieces[0].astype(f32)
    for far in range(1, FAR):
        rows += pieces[far].astype(f32)
    sums = rows[OWN : OWN + 8]
    degree = 1.0 + (sums[0:2] + sums[2:4])
    scale = jnp.concatenate([lax.rsqrt(degree), jnp.zeros((BLK - 2, BLK), f32)], axis=0).T
    halves = [scale[(h % 2) * HALF : (h % 2 + 1) * HALF, h // 2 : h // 2 + 1] for h in range(4)]
    for part in range(OWN // HALF):
        factor = jnp.where(odd[0] == 1, halves[part + 1], halves[part])
        piece = rows[part * HALF : (part + 1) * HALF] * factor
        out[part * HALF : (part + 1) * HALF] = jnp.maximum(piece, 0.0).astype(bf16)


def params(mebibytes=32):
    return pltpu.CompilerParams(vmem_limit_bytes=mebibytes * 1024 * 1024)


def shards(features, weight, block_values, block_coords, block_counts):
    coords = block_coords.T
    core = (lax.axis_index("row") % 2).astype(jnp.int32).reshape(1)
    odd = (lax.axis_index("col") % 2).astype(jnp.int32).reshape(1)

    outgoing = pl.pallas_call(
        column_sums_kernel,
        out_shape=jax.ShapeDtypeStruct((CHIPS, GATHER_ROWS, F), bf16),
        in_specs=[HBM, HBM, HBM, HBM],
        out_specs=VMEM,
        scratch_shapes=[
            pltpu.SMEM((1,), jnp.int32),
            pltpu.SMEM((2, SLOTS), jnp.int32),
            pltpu.VMEM((SLOTS, BLK, BLK), bf16),
            pltpu.VMEM((OWN, F), bf16),
            pltpu.VMEM((32, BLK), f32),
            pltpu.SemaphoreType.DMA((3,)),
            pltpu.SemaphoreType.DMA((SLOTS // UNROLL,)),
        ],
        compiler_params=params(60),
    )(block_counts, coords, block_values, features)
    mine = lax.all_to_all(outgoing, "row", 0, 0, axis_index_groups=CHIP_GROUPS, tiled=True)
    other = lax.ppermute(mine, "row", [(r, r ^ 1) for r in range(N_ROW)])

    row_sums = pl.pallas_call(
        row_sums_kernel,
        out_shape=jax.ShapeDtypeStruct((NEAR, 4 * FAR, BLK), bf16),
        in_specs=[HBM, SMEM, SMEM, VMEM],
        out_specs=VMEM,
        scratch_shapes=[pltpu.VMEM((BLK, BLK), f32)],
        compiler_params=params(),
        cost_estimate=pl.CostEstimate(flops=2 * SLOTS * BLK**3, bytes_accessed=2 * SLOTS * BLK**2, transcendentals=0),
    )(mine, block_counts, coords, block_values)

    partial = pl.pallas_call(
        aggregate_kernel,
        out_shape=jax.ShapeDtypeStruct((NEAR, NEAR_ROWS, F), bf16),
        in_specs=[SMEM, SMEM, SMEM, VMEM, VMEM, VMEM, VMEM, VMEM],
        out_specs=VMEM,
        scratch_shapes=[
            pltpu.VMEM((BLK, BLK), f32),
            pltpu.VMEM((COL_BLOCKS * BLK, F), bf16),
            pltpu.VMEM(((ROW_BLOCKS + 1) * BLK, F), f32),
        ],
        compiler_params=params(),
    )(core, block_counts, coords, mine, other, weight, block_values, row_sums)
    partial = lax.all_to_all(partial, ("row", "col"), 0, 0, axis_index_groups=near_groups(), tiled=True)

    reduced = pl.pallas_call(
        near_kernel,
        out_shape=jax.ShapeDtypeStruct((FAR, FAR_ROWS, F), bf16),
        in_specs=[VMEM],
        out_specs=VMEM,
        compiler_params=params(),
    )(partial)
    reduced = lax.all_to_all(reduced, "col", 0, 0, axis_index_groups=FAR_GROUPS, tiled=True)

    return pl.pallas_call(
        far_kernel,
        out_shape=jax.ShapeDtypeStruct((OWN, F), bf16),
        in_specs=[SMEM, VMEM],
        out_specs=VMEM,
        compiler_params=params(),
    )(odd, reduced)


def solution(mesh):
    return jax.shard_map(
        shards,
        mesh=mesh,
        in_specs=(
            P(("col", "row"), None),
            P(),
            P(("row", "col"), None, None),
            P(("row", "col"), None),
            P(("row", "col")),
        ),
        out_specs=P(("row", "col"), None),
        check_vma=False,
    )
```

```python
import jax
import jax.numpy as jnp
from jax import lax
from jax.experimental import pallas as pl
from jax.experimental.pallas import tpu as pltpu
from jax.sharding import PartitionSpec as P

F = 128
BLK = 128
SLOTS = 64
ROW_BLOCKS = 48
COL_BLOCKS = 24
OWN = 192
N_ROW = 16
N_COL = 32
CHIPS = N_ROW // 2
NEAR = 4
FAR = N_COL // NEAR
HALF = 64
UNROLL = 8
BATCH = 32

GATHER_ROWS = OWN + COL_BLOCKS
NEAR_ROWS = FAR * OWN + 4 * FAR
FAR_ROWS = OWN + 8

CHIP_TURN = 5
FAR_TURN = 5


def owner(near, far):
    return NEAR * ((far + FAR_TURN) % FAR) + near


CHIP_GROUPS = [[2 * ((m + CHIP_TURN) % CHIPS) + core for m in range(CHIPS)] for core in range(2)]


def near_groups():
    groups = []
    for row in range(N_ROW):
        for far in range(FAR):
            even = (far + row % 2) % FAR
            zs = (2 * even, 2 * far + 1)
            groups.append([row * N_COL + 2 * zs[near // 2] + near % 2 for near in range(NEAR)])
    return groups


FAR_GROUPS = [[owner(near, far) for far in range(FAR)] for near in range(NEAR)]

VMEM = pl.BlockSpec(memory_space=pltpu.VMEM)
SMEM = pl.BlockSpec(memory_space=pltpu.SMEM)
HBM = pl.BlockSpec(memory_space=pltpu.HBM)
f32 = jnp.float32
bf16 = jnp.bfloat16


def split(value):
    high = value.astype(bf16).astype(f32)
    return high, value - high


def column_sums_kernel(counts_in, coords_in, values_in, features_in, out, counts, coords, values, features, sums, small_sems, sems):
    small = [
        pltpu.make_async_copy(counts_in, counts, small_sems.at[0]),
        pltpu.make_async_copy(coords_in, coords, small_sems.at[1]),
        pltpu.make_async_copy(features_in, features, small_sems.at[2]),
    ]
    for copy in small:
        copy.start()
    chunks = []
    for group in range(SLOTS // UNROLL):
        slots = pl.ds(group * UNROLL, UNROLL)
        chunks.append(pltpu.make_async_copy(values_in.at[slots], values.at[slots], sems.at[group]))
        chunks[-1].start()
    sums[...] = jnp.zeros_like(sums)
    small[2].wait()
    for m in range(CHIPS):
        out[m, :OWN] = features[...]
    small[0].wait()
    small[1].wait()
    live = counts[0]
    for group in range(SLOTS // UNROLL):
        chunks[group].wait()

        @pl.when(group * UNROLL < live)
        def _():
            for step in range(UNROLL):
                slot = group * UNROLL + step
                col = jnp.where(slot < live, coords[1, slot], COL_BLOCKS)
                sums[pl.ds(col, 1), :] += jnp.sum(values[slot].astype(f32), axis=0, keepdims=True)

    for m in range(CHIPS):
        out[m, OWN:] = sums[:COL_BLOCKS].astype(bf16)


def row_sums_kernel(mine, counts, coords, values, out, sums):
    live = counts[0]
    sums[...] = jnp.zeros_like(sums)
    lane = lax.broadcasted_iota(jnp.int32, (BLK, BLK), 1)

    @pl.loop(0, lax.div(live + BATCH - 1, BATCH))
    def _(group):
        added = sums[...]
        for step in range(BATCH):
            slot = group * BATCH + step
            row = jnp.where(slot < live, coords[0, slot], ROW_BLOCKS)
            picked = (lane == row).astype(f32).astype(bf16)
            added += jnp.dot(values[slot], picked, preferred_element_type=f32)
        sums[...] = added

    high, low = split(sums[...].T)
    for near in range(NEAR):
        picks = []
        for part in (high, low):
            for far in range(FAR):
                first = owner(near, far) * OWN // BLK
                picks.append(part[first : first + 2])
        out[near] = jnp.concatenate(picks, axis=0).astype(bf16)


def aggregate_kernel(core, counts, coords, mine, other, weight, values, row_sums, out, scales, scaled, total):
    live = counts[0]
    sums = jnp.zeros((COL_BLOCKS, BLK), f32)
    for m in range(CHIPS):
        sums += mine[m, OWN:].astype(f32) + other[m, OWN:].astype(f32)
    degree = 1.0 + sums
    scales[...] = jnp.zeros_like(scales)
    scales[:COL_BLOCKS] = lax.rsqrt(degree)
    scales[...] = scales[...].T

    def scale(pieces):
        for r in range(N_ROW):
            transformed = jnp.dot(pieces[r % 2][(r // 2 - CHIP_TURN) % CHIPS, :OWN], weight[...], preferred_element_type=f32)
            for part in range(OWN // HALF):
                h = r * (OWN // HALF) + part
                factor = scales[(h % 2) * HALF : (h % 2 + 1) * HALF, h // 2 : h // 2 + 1]
                rows = transformed[part * HALF : (part + 1) * HALF]
                scaled[h * HALF : (h + 1) * HALF] = (rows * factor).astype(bf16)

    @pl.when(core[0] == 0)
    def _():
        scale((mine, other))

    @pl.when(core[0] == 1)
    def _():
        scale((other, mine))

    total[...] = jnp.zeros_like(total)

    @pl.loop(0, lax.div(live + BATCH - 1, BATCH))
    def _(group):
        rows, products = [], []
        for step in range(BATCH):
            slot = group * BATCH + step
            alive = slot < live
            row = jnp.where(alive, coords[0, slot], ROW_BLOCKS)
            col = jnp.where(alive, coords[1, slot], 0)
            picked = scaled[pl.ds(pl.multiple_of(col * BLK, BLK), BLK), :]
            rows.append(row)
            products.append(jnp.dot(values[slot], picked, preferred_element_type=f32))
        for row, product in zip(rows, products):
            total[pl.ds(pl.multiple_of(row * BLK, BLK), BLK), :] += product

    for near in range(NEAR):
        for far in range(FAR):
            dest = owner(near, far)
            out[near, far * OWN : (far + 1) * OWN] = total[dest * OWN : (dest + 1) * OWN].astype(bf16)
        out[near, FAR * OWN :] = row_sums[near]


def near_kernel(pieces, out):
    sums = pieces[0, FAR * OWN :].astype(f32)
    for near in range(1, NEAR):
        sums += pieces[near, FAR * OWN :].astype(f32)
    high, low = split(sums[: 2 * FAR] + sums[2 * FAR :])
    for far in range(FAR):
        rows = pieces[0, far * OWN : (far + 1) * OWN].astype(f32)
        for near in range(1, NEAR):
            rows += pieces[near, far * OWN : (far + 1) * OWN].astype(f32)
        pair = slice(2 * far, 2 * far + 2)
        tail = jnp.concatenate([high[pair], low[pair], jnp.zeros((4, BLK), f32)], axis=0)
        out[far] = jnp.concatenate([rows, tail], axis=0).astype(bf16)


def far_kernel(odd, pieces, out):
    rows = pieces[0].astype(f32)
    for far in range(1, FAR):
        rows += pieces[far].astype(f32)
    sums = rows[OWN : OWN + 8]
    degree = 1.0 + (sums[0:2] + sums[2:4])
    scale = jnp.concatenate([lax.rsqrt(degree), jnp.zeros((BLK - 2, BLK), f32)], axis=0).T
    halves = [scale[(h % 2) * HALF : (h % 2 + 1) * HALF, h // 2 : h // 2 + 1] for h in range(4)]
    for part in range(OWN // HALF):
        factor = jnp.where(odd[0] == 1, halves[part + 1], halves[part])
        piece = rows[part * HALF : (part + 1) * HALF] * factor
        out[part * HALF : (part + 1) * HALF] = jnp.maximum(piece, 0.0).astype(bf16)


def params(mebibytes=32):
    return pltpu.CompilerParams(vmem_limit_bytes=mebibytes * 1024 * 1024)


def shards(features, weight, block_values, block_coords, block_counts):
    coords = block_coords.T
    core = (lax.axis_index("row") % 2).astype(jnp.int32).reshape(1)
    odd = (lax.axis_index("col") % 2).astype(jnp.int32).reshape(1)

    outgoing = pl.pallas_call(
        column_sums_kernel,
        out_shape=jax.ShapeDtypeStruct((CHIPS, GATHER_ROWS, F), bf16),
        in_specs=[HBM, HBM, HBM, HBM],
        out_specs=VMEM,
        scratch_shapes=[
            pltpu.SMEM((1,), jnp.int32),
            pltpu.SMEM((2, SLOTS), jnp.int32),
            pltpu.VMEM((SLOTS, BLK, BLK), bf16),
            pltpu.VMEM((OWN, F), bf16),
            pltpu.VMEM((32, BLK), f32),
            pltpu.SemaphoreType.DMA((3,)),
            pltpu.SemaphoreType.DMA((SLOTS // UNROLL,)),
        ],
        compiler_params=params(60),
    )(block_counts, coords, block_values, features)
    mine = lax.all_to_all(outgoing, "row", 0, 0, axis_index_groups=CHIP_GROUPS, tiled=True)
    other = lax.ppermute(mine, "row", [(r, r ^ 1) for r in range(N_ROW)])

    row_sums = pl.pallas_call(
        row_sums_kernel,
        out_shape=jax.ShapeDtypeStruct((NEAR, 4 * FAR, BLK), bf16),
        in_specs=[HBM, SMEM, SMEM, VMEM],
        out_specs=VMEM,
        scratch_shapes=[pltpu.VMEM((BLK, BLK), f32)],
        compiler_params=params(),
        cost_estimate=pl.CostEstimate(flops=2 * SLOTS * BLK**3, bytes_accessed=2 * SLOTS * BLK**2, transcendentals=0),
    )(mine, block_counts, coords, block_values)

    partial = pl.pallas_call(
        aggregate_kernel,
        out_shape=jax.ShapeDtypeStruct((NEAR, NEAR_ROWS, F), bf16),
        in_specs=[SMEM, SMEM, SMEM, VMEM, VMEM, VMEM, VMEM, VMEM],
        out_specs=VMEM,
        scratch_shapes=[
            pltpu.VMEM((BLK, BLK), f32),
            pltpu.VMEM((COL_BLOCKS * BLK, F), bf16),
            pltpu.VMEM(((ROW_BLOCKS + 1) * BLK, F), f32),
        ],
        compiler_params=params(),
    )(core, block_counts, coords, mine, other, weight, block_values, row_sums)
    partial = lax.all_to_all(partial, ("row", "col"), 0, 0, axis_index_groups=near_groups(), tiled=True)

    reduced = pl.pallas_call(
        near_kernel,
        out_shape=jax.ShapeDtypeStruct((FAR, FAR_ROWS, F), bf16),
        in_specs=[VMEM],
        out_specs=VMEM,
        compiler_params=params(),
    )(partial)
    reduced = lax.all_to_all(reduced, "col", 0, 0, axis_index_groups=FAR_GROUPS, tiled=True)

    return pl.pallas_call(
        far_kernel,
        out_shape=jax.ShapeDtypeStruct((OWN, F), bf16),
        in_specs=[SMEM, VMEM],
        out_specs=VMEM,
        compiler_params=params(),
    )(odd, reduced)


def solution(mesh):
    return jax.shard_map(
        shards,
        mesh=mesh,
        in_specs=(
            P(("col", "row"), None),
            P(),
            P(("row", "col"), None, None),
            P(("row", "col"), None),
            P(("row", "col")),
        ),
        out_specs=P(("row", "col"), None),
        check_vma=False,
    )
```
